32 devices in a mesh: groups: 2 (over y), expert: 2 (over x), tensor: 4 (over z), replica: 2 (over core).
Axes of the slice: x: 2, y: 2, z: 4, core: 2. Of those that a mesh axis runs over, the one named last changes fastest.
Arguments:
- tokens: bfloat16 [2048, 3072], P(('groups', 'replica'), 'tensor'), parts along dimension 0, may hold values from -6 to 6
- w_gate: bfloat16 [4, 3072, 16384], P('expert', 'replica', 'tensor'), may hold values from -0.109375 to 0.109375
- w_up: bfloat16 [4, 3072, 16384], P('expert', 'replica', 'tensor'), may hold values from -0.109375 to 0.109375
- w_down: bfloat16 [4, 16384, 3072], P('expert', 'tensor', 'replica'), may hold values from -0.0625 to 0.0625
- block_rows: int32 [4, 4, 512], P('expert', ('groups', 'replica')), parts along dimension 1, may hold values from 0 to 511, as said below
- block_gates: float32 [4, 4, 512], P('expert', ('groups', 'replica')), parts along dimension 1, may hold values from 0 to 1, as said below
- block_count: int32 [4, 4], P('expert', ('groups', 'replica')), parts along dimension 1, may hold values from 1 to 4, as said below
Outputs:
- moe_output: bfloat16 [2048, 3072], P(('groups', 'replica'), 'tensor'), parts along dimension 0
The draws below stay inside these ranges and needn't reach their ends.
There are 2 independent parts, one for each index of `groups`. The reference program is written for one: setup_inputs(seed, part) draws one part's arguments, and reference() takes and returns one part's arrays. A program takes and returns all parts, laid end to end along the dimension named above; an argument that names none is the same for every part. Nothing has to cross between parts.
Inputs may be any that keep to these rules, and one draw needn't show every extreme that they name: `block_rows`: for each expert e and replica index r, the first slots of the list name the index, among the 512 tokens of replica index r, of tokens routed to e, all distinct; every such token is named so by exactly 2 experts. The rows end inside the last counted block; the remaining slots of that block and all slots past the count hold arbitrary indices. `block_gates`: positive on an expert's rows, 0 on the slots after its rows inside its last counted block, arbitrary past the count. `block_count`: for each replica index some expert has exactly 4 counted blocks; for each expert the counts over the 2 replica indices add up to at most 6, and some expert reaches that total.
All inputs are finite; a program needn't handle non-finite values.
Results may differ from the reference program's by a relative error of at most 0.013.
Values may be sent and summed in bfloat16 or wider, within the bound.
A program may use at most 448 MiB of HBM per device.

```python
import jax
import jax.numpy as jnp
from jax import lax

D = 3072
FF = 16384
EXPERTS = 4
BLOCK = 128
TOK_DEV = 512
SLOTS = 512
TOKENS = 1024
FF_DEV = 4096
N_TENSOR = 4
N_REPLICA = 2


def routing_plan(key):
    expert_order = jax.random.permutation(jax.random.fold_in(key, 11), EXPERTS)
    id_list = []
    load_list = []
    count_list = []
    slot_index = jnp.arange(SLOTS, dtype=jnp.int32)
    for replica_idx in range(N_REPLICA):
        rest_rows = jax.random.randint(jax.random.fold_in(key, 20 + replica_idx), (), TOK_DEV // 16, 7 * TOK_DEV // 16 + 1).astype(jnp.int32)
        first_load = TOK_DEV if replica_idx % 2 == 0 else TOK_DEV // 2
        second_load = TOK_DEV // 2 if replica_idx % 2 == 0 else TOK_DEV
        ranked = jnp.stack([jnp.int32(first_load), jnp.int32(second_load), rest_rows, jnp.int32(TOK_DEV // 2) - rest_rows]).astype(jnp.int32)
        row_loads = jnp.zeros((EXPERTS,), jnp.int32).at[expert_order].set(ranked)
        token_order = jax.random.permutation(jax.random.fold_in(key, 30 + replica_idx), TOK_DEV).astype(jnp.int32)
        sequence = jnp.concatenate([token_order, token_order])
        offsets = jnp.cumsum(row_loads) - row_loads
        position = jnp.clip(offsets[:, None] + slot_index[None, :], 0, 2 * TOK_DEV - 1)
        routed_ids = sequence[position]
        filler = jax.random.randint(jax.random.fold_in(key, 40 + replica_idx), (EXPERTS, SLOTS), 0, TOK_DEV).astype(jnp.int32)
        id_list.append(jnp.where(slot_index[None, :] < row_loads[:, None], routed_ids, filler))
        load_list.append(row_loads)
        count_list.append((row_loads + BLOCK - 1) // BLOCK)
    return (jnp.stack(id_list, axis=1), jnp.stack(load_list, axis=1), jnp.stack(count_list, axis=1))


def draw_block_rows(key, part):
    token_ids, row_loads, counts = routing_plan(key)
    return token_ids.astype(jnp.int32)


def draw_block_count(key, part):
    token_ids, row_loads, counts = routing_plan(key)
    return counts.astype(jnp.int32)


def draw_block_gates(key, part):
    token_ids, row_loads, counts = routing_plan(key)
    key = jax.random.fold_in(key, 3)
    values = jax.random.uniform(key, (EXPERTS, N_REPLICA, SLOTS), jnp.float32, 0.25, 1.0)
    slot_index = jnp.arange(SLOTS, dtype=jnp.int32)[None, None, :]
    padding = (slot_index >= row_loads[:, :, None]) & (slot_index < counts[:, :, None] * BLOCK)
    return jnp.where(padding, jnp.float32(0.0), values).astype(jnp.float32)


def spiked(array, rng, source, target, parts, factor):
    def block_of(dim):
        return (jnp.arange(array.shape[dim]) // (array.shape[dim] // parts)).reshape((-1,) + (1,) * (array.ndim - 1 - dim))

    one_side = jax.random.permutation(rng, parts)[block_of(target)]
    second = (block_of(target) + parts // 2) % parts
    return jnp.where((block_of(source) == one_side) | (block_of(source) == second), factor * array, array)


def level_of(rng, extent, pieces, smallest, largest):
    gain, own = 1.0, jax.random.fold_in(rng, 6)
    for axis_at, parts in pieces:
        heights = jnp.exp(jax.random.uniform(jax.random.fold_in(own, axis_at), (parts,), jnp.float32, smallest / len(pieces), largest / len(pieces)))
        gain = gain * jnp.repeat(heights, extent[axis_at] // parts).reshape([-1 if axis == axis_at else 1 for axis in range(len(extent))])
    return gain


def centred(rng, shape, scale, limit, cuts=(), kind=jnp.bfloat16):
    values = scale * jax.random.normal(rng, shape, jnp.float32)
    if cuts:
        values = values * level_of(rng, shape, cuts, -0.22, 0.18)
    return jnp.clip(values, -limit, limit).astype(kind)


def gaussian_with(rng, extent, deviation, most, split, heavy, kind=jnp.bfloat16):
    array = deviation * jax.random.normal(rng, extent, jnp.float32)
    if split:
        array = array * level_of(rng, extent, split, -0.22, 0.18)
    return jnp.clip(spiked(array, jax.random.fold_in(rng, 3), *heavy), -most, most).astype(kind)


def setup_inputs(seed: int = 0, part: int = 0) -> dict:
    streams_of = jax.random.split(jax.random.key(seed), 8)
    part_splits = jax.random.split(jax.random.fold_in(streams_of[7], part), 8)
    tokens = centred(part_splits[0], (TOKENS, D), 1.0, 6.0, ((0, 2), (1, 4)))
    w_gate = centred(streams_of[1], (EXPERTS, D, FF), D ** -0.5, 0.109375, ((0, 2), (1, 2), (2, 4)))
    w_up = centred(streams_of[2], (EXPERTS, D, FF), D ** -0.5, 0.109375, ((0, 2), (1, 2), (2, 4)))
    w_down = gaussian_with(streams_of[3], (EXPERTS, FF, D), FF ** -0.5, 0.0625, ((0, 2), (1, 4), (2, 2)), (1, 2, 4, 2.0))
    block_rows = draw_block_rows(jax.random.fold_in(jax.random.fold_in(streams_of[7], part), 71), part)
    block_gates = draw_block_gates(jax.random.fold_in(jax.random.fold_in(streams_of[7], part), 71), part)
    block_count = draw_block_count(jax.random.fold_in(jax.random.fold_in(streams_of[7], part), 71), part)
    return dict(tokens=tokens, w_gate=w_gate, w_up=w_up, w_down=w_down, block_rows=block_rows, block_gates=block_gates, block_count=block_count)


def expert_rows(routed, gate_matrix, up_matrix, down_matrix):
    gate_acts = jnp.dot(routed, gate_matrix, preferred_element_type=jnp.float32)
    up_acts = jnp.dot(routed, up_matrix, preferred_element_type=jnp.float32)
    hidden = (jax.nn.silu(gate_acts) * up_acts).astype(jnp.bfloat16)

    def add_group(group_index, summed):
        offset = (group_index * FF_DEV).astype(jnp.int32)
        hidden_part = lax.dynamic_slice_in_dim(hidden, offset, FF_DEV, 1)
        down_part = lax.dynamic_slice_in_dim(down_matrix, offset, FF_DEV, 0)
        group_part = jnp.dot(hidden_part, down_part, preferred_element_type=jnp.float32)
        group_part = lax.optimization_barrier(group_part.astype(jnp.bfloat16))
        return summed + group_part.astype(jnp.float32)

    zeros_start = jnp.zeros((routed.shape[0], down_matrix.shape[1]), jnp.float32)
    return lax.fori_loop(0, N_TENSOR, add_group, zeros_start)


def reference(tokens, w_gate, w_up, w_down, block_rows, block_gates, block_count):
    result = jnp.zeros((TOKENS, D), jnp.float32)
    slot_index = jnp.arange(SLOTS, dtype=jnp.int32)
    for expert_idx in range(EXPERTS):
        for replica_idx in range(N_REPLICA):
            counted = slot_index < BLOCK * block_count[expert_idx, replica_idx]
            slot_weight = jnp.where(counted, block_gates[expert_idx, replica_idx], jnp.float32(0.0))
            token_ids = (replica_idx * TOK_DEV + block_rows[expert_idx, replica_idx]).astype(jnp.int32)
            routed = jnp.take(tokens, token_ids, axis=0)
            expert_out = expert_rows(routed, w_gate[expert_idx], w_up[expert_idx], w_down[expert_idx])
            result = result.at[token_ids].add(slot_weight[:, None] * expert_out)
    return result.astype(jnp.bfloat16)
```

```python
import jax
import jax.numpy as jnp
from jax import lax
from jax.sharding import PartitionSpec as P

BLOCK = 128
PAIR_BLOCKS = 6
SWAP = ((0, 1), (1, 0))


def swap_cores(x):
    return lax.ppermute(x, "replica", SWAP)


def half_of(x, axis, which):
    size = x.shape[axis] // 2
    return lax.dynamic_slice_in_dim(x, which * size, size, axis)


def dot(a, b):
    return jnp.dot(a, b, preferred_element_type=jnp.float32)


def slot_lists(block_rows, block_gates, block_count, core, token_rows):
    experts, _, slots = block_rows.shape
    blocks = slots // BLOCK
    counts = jnp.broadcast_to(block_count.astype(jnp.float32)[:, :, None], block_rows.shape)
    mine = jnp.concatenate([block_rows.astype(jnp.float32), block_gates, counts], axis=1)
    other = swap_cores(mine)
    first = jnp.where(core == 0, mine, other)
    second = jnp.where(core == 0, other, mine)
    shift = jnp.float32(token_rows)
    first_rows = first[:, 0] + jnp.where(core == 0, 0.0, shift)
    second_rows = second[:, 0] + jnp.where(core == 0, shift, 0.0)
    rows = jnp.concatenate([first_rows, second_rows], axis=1).reshape(experts, 1, 2 * blocks, BLOCK)
    gates = jnp.concatenate([first[:, 1], second[:, 1]], axis=1).reshape(experts, 1, 2 * blocks, BLOCK)
    n_first = first[:, 2, :1].astype(jnp.int32)
    n_second = second[:, 2, :1].astype(jnp.int32)
    at = jnp.arange(PAIR_BLOCKS, dtype=jnp.int32)[None, :]
    source = jnp.where(at < n_first, at, blocks + at - n_first)
    source = jnp.where(at < n_first + n_second, source, -1)
    pick = source[:, :, None] == jnp.arange(2 * blocks, dtype=jnp.int32)[None, None, :]
    pick = pick[:, :, :, None]
    ids = jnp.sum(jnp.where(pick, rows, 0.0), axis=2).reshape(experts, PAIR_BLOCKS * BLOCK)
    weight = jnp.sum(jnp.where(pick, gates, 0.0), axis=2).reshape(experts, PAIR_BLOCKS * BLOCK)
    return ids.astype(jnp.int32), weight


def body(tokens, w_gate, w_up, w_down, block_rows, block_gates, block_count):
    core = lax.axis_index("replica")
    token_rows = tokens.shape[0]
    experts = w_gate.shape[0]
    ids, weight = slot_lists(block_rows, block_gates, block_count, core, token_rows)
    full_rows = lax.all_gather(tokens, "tensor", axis=1, tiled=True)
    from_other = swap_cores(half_of(full_rows, 1, 1 - core))
    table = jnp.concatenate([half_of(full_rows, 1, core), from_other], axis=0)
    token_at = jnp.arange(2 * token_rows, dtype=jnp.int32)

    kept, arriving = [], []
    routed_all = []
    for e in range(experts):
        onehot = (ids[e][:, None] == token_at[None, :]).astype(jnp.bfloat16)
        routed = dot(onehot, table).astype(jnp.bfloat16)
        routed_all.append(routed)
        sent = [swap_cores(dot(routed, half_of(w[e], 1, 1 - core)).astype(jnp.bfloat16)) for w in (w_gate, w_up)]
        arriving.append(sent)
        kept.append([dot(routed, half_of(w[e], 1, core)) for w in (w_gate, w_up)])
    hidden, hidden_other = [], []
    for e in range(experts):
        gate = kept[e][0] + arriving[e][0].astype(jnp.float32)
        up = kept[e][1] + arriving[e][1].astype(jnp.float32)
        hidden.append((jax.nn.silu(gate) * up).astype(jnp.bfloat16))
        hidden_other.append(swap_cores(hidden[e]))
    parts = []
    for e in range(experts):
        out = dot(hidden[e], half_of(w_down[e], 0, core))
        out = out + dot(hidden_other[e], half_of(w_down[e], 0, 1 - core))
        parts.append((out * weight[e][:, None]).astype(jnp.bfloat16))
    parts = jnp.concatenate(parts, axis=0)
    spread = (token_at[:, None] == ids.reshape(-1)[None, :]).astype(jnp.bfloat16)
    mine = dot(spread[:token_rows], parts).astype(jnp.bfloat16)
    theirs = swap_cores(dot(spread[token_rows:], parts).astype(jnp.bfloat16))
    low = jnp.where(core == 0, mine, theirs)
    high = jnp.where(core == 0, theirs, mine)
    whole = jnp.concatenate([low, high], axis=1)
    own = lax.psum_scatter(whole, "tensor", scatter_dimension=1, tiled=True)
    if lax.axis_size("expert") == 2:
        across = lax.ppermute(own, "expert", SWAP)
        return (own.astype(jnp.float32) + across.astype(jnp.float32)).astype(jnp.bfloat16)
    return lax.psum(own, "expert")


def solution(mesh):
    placed = (
        P(("groups", "replica"), "tensor"),
        P("expert", "replica", "tensor"),
        P("expert", "replica", "tensor"),
        P("expert", "tensor", "replica"),
        P("expert", ("groups", "replica"), None),
        P("expert", ("groups", "replica"), None),
        P("expert", ("groups", "replica")),
    )
    return jax.shard_map(
        body,
        mesh=mesh,
        in_specs=placed,
        out_specs=P(("groups", "replica"), "tensor"),
        check_vma=False,
    )
```

```python
import functools

import jax
import jax.numpy as jnp
from jax import lax
from jax.experimental import pallas as pl
from jax.experimental.pallas import tpu as pltpu
from jax.sharding import PartitionSpec as P

BLOCK = 128
TILE = 512
VMEM_BYTES = 48 * 1024 * 1024
MESH = pl.DeviceIdType.MESH
PAIR_BLOCKS = 6
SWAP = ((0, 1), (1, 0))


def swap_cores(x):
    return lax.ppermute(x, "replica", SWAP)


def half_of(x, axis, which):
    size = x.shape[axis] // 2
    return lax.dynamic_slice_in_dim(x, which * size, size, axis)


def dot(a, b):
    return jnp.dot(a, b, preferred_element_type=jnp.float32)


def slot_lists(block_rows, block_gates, block_count, core, token_rows):
    experts, _, slots = block_rows.shape
    blocks = slots // BLOCK
    counts = jnp.broadcast_to(block_count.astype(jnp.float32)[:, :, None], block_rows.shape)
    mine = jnp.concatenate([block_rows.astype(jnp.float32), block_gates, counts], axis=1)
    other = swap_cores(mine)
    first = jnp.where(core == 0, mine, other)
    second = jnp.where(core == 0, other, mine)
    shift = jnp.float32(token_rows)
    first_rows = first[:, 0]
    second_rows = second[:, 0] + shift
    rows = jnp.concatenate([first_rows, second_rows], axis=1).reshape(experts, 1, 2 * blocks, BLOCK)
    gates = jnp.concatenate([first[:, 1], second[:, 1]], axis=1).reshape(experts, 1, 2 * blocks, BLOCK)
    n_first = first[:, 2, :1].astype(jnp.int32)
    n_second = second[:, 2, :1].astype(jnp.int32)
    at = jnp.arange(PAIR_BLOCKS, dtype=jnp.int32)[None, :]
    source = jnp.where(at < n_first, at, blocks + at - n_first)
    source = jnp.where(at < n_first + n_second, source, -1)
    pick = source[:, :, None] == jnp.arange(2 * blocks, dtype=jnp.int32)[None, None, :]
    pick = pick[:, :, :, None]
    ids = jnp.sum(jnp.where(pick, rows, 0.0), axis=2).reshape(experts, PAIR_BLOCKS * BLOCK)
    weight = jnp.sum(jnp.where(pick, gates, 0.0), axis=2).reshape(experts, PAIR_BLOCKS * BLOCK)
    return ids.astype(jnp.int32), weight


def weight_spec(shape, e, split, which):
    if split == 2:
        tile = min(TILE, shape[2] // 2)
        per = shape[2] // 2 // tile
        return pl.BlockSpec(
            (1, shape[1], tile),
            lambda j, at: (e, 0, (at[0] if which else 1 - at[0]) * per + j),
        )
    tile = min(TILE, shape[2])
    return pl.BlockSpec((1, shape[1] // 2, tile), lambda j, at: (e, at[0] if which else 1 - at[0], j))


def whole_spec(x):
    return pl.BlockSpec(x.shape, lambda j, at: (0,) * len(x.shape))


def tiles_spec(rows, tile):
    return pl.BlockSpec((rows, tile), lambda j, at: (0, j))


def cost(rows, depth, columns):
    return pl.CostEstimate(
        flops=2 * rows * depth * columns,
        bytes_accessed=2 * (rows * depth + depth * columns + rows * columns),
        transcendentals=0,
    )


def compiler_params(**more):
    return pltpu.CompilerParams(vmem_limit_bytes=VMEM_BYTES, **more)


def partial_kernel(at, routed, gate_matrix, up_matrix, gate_out, up_out):
    gate_out[...] = dot(routed[...], gate_matrix[0]).astype(jnp.bfloat16)
    up_out[...] = dot(routed[...], up_matrix[0]).astype(jnp.bfloat16)


def partial_sums(at, routed, w_gate, w_up, e):
    rows, depth = routed.shape
    half = w_gate.shape[2] // 2
    tile = min(TILE, half)
    out = jax.ShapeDtypeStruct((rows, half), jnp.bfloat16)
    return pl.pallas_call(
        partial_kernel,
        grid_spec=pltpu.PrefetchScalarGridSpec(
            num_scalar_prefetch=1,
            grid=(half // tile,),
            in_specs=[whole_spec(routed), weight_spec(w_gate.shape, e, 2, 0), weight_spec(w_up.shape, e, 2, 0)],
            out_specs=[tiles_spec(rows, tile)] * 2,
        ),
        out_shape=[out, out],
        cost_estimate=cost(rows, depth, 2 * half),
        compiler_params=compiler_params(),
    )(at, routed, w_gate, w_up)


def hidden_kernel(at, routed, gate_matrix, up_matrix, gate_in, up_in, out):
    gate = dot(routed[...], gate_matrix[0]) + gate_in[...].astype(jnp.float32)
    up = dot(routed[...], up_matrix[0]) + up_in[...].astype(jnp.float32)
    out[...] = (gate / (1.0 + jnp.exp(-gate)) * up).astype(jnp.bfloat16)


def hidden_units(at, routed, w_gate, w_up, gate_in, up_in, e):
    rows, depth = routed.shape
    half = w_gate.shape[2] // 2
    tile = min(TILE, half)
    return pl.pallas_call(
        hidden_kernel,
        grid_spec=pltpu.PrefetchScalarGridSpec(
            num_scalar_prefetch=1,
            grid=(half // tile,),
            in_specs=[whole_spec(routed), weight_spec(w_gate.shape, e, 2, 1), weight_spec(w_up.shape, e, 2, 1)]
            + [tiles_spec(rows, tile)] * 2,
            out_specs=tiles_spec(rows, tile),
        ),
        out_shape=jax.ShapeDtypeStruct((rows, half), jnp.bfloat16),
        cost_estimate=cost(rows, depth, 2 * half),
        compiler_params=compiler_params(),
    )(at, routed, w_gate, w_up, gate_in, up_in)


def down_kernel(at, own, other, own_matrix, other_matrix, weight, out):
    summed = dot(own[...], own_matrix[0]) + dot(other[...], other_matrix[0])
    out[...] = (summed * weight[...]).astype(jnp.bfloat16)


def weighted_down(at, own, other, w_down, weight, e):
    rows, half = own.shape
    columns = w_down.shape[2]
    tile = min(TILE, columns)
    return pl.pallas_call(
        down_kernel,
        grid_spec=pltpu.PrefetchScalarGridSpec(
            num_scalar_prefetch=1,
            grid=(columns // tile,),
            in_specs=[
                whole_spec(own),
                whole_spec(other),
                weight_spec(w_down.shape, e, 1, 1),
                weight_spec(w_down.shape, e, 1, 0),
                whole_spec(weight),
            ],
            out_specs=tiles_spec(rows, tile),
        ),
        out_shape=jax.ShapeDtypeStruct((rows, columns), jnp.bfloat16),
        cost_estimate=cost(rows, 2 * half, columns),
        compiler_params=compiler_params(),
    )(at, own, other, w_down, w_down, weight)


def meet(x, z, r, n_tensor):
    barrier = pltpu.get_barrier_semaphore()
    for dz in range(n_tensor):
        for dr in range(2):
            if dz or dr:
                there = {"tensor": lax.rem(z + dz, n_tensor), "replica": lax.rem(r + dr, 2)}
                pl.semaphore_signal(barrier, inc=1, device_id=there, device_id_type=MESH)
    pl.semaphore_signal(barrier, inc=1, device_id={"expert": 1 - x}, device_id_type=MESH)
    pl.semaphore_wait(barrier, 2 * n_tensor)


def rows_at(start, size):
    return pl.ds(pl.multiple_of(start, 64), size)


def gather_kernel(n, pieces, tok, table, own_sem, own_send, own_recv, z_send, z_recv, x_send, x_recv):
    x, z, r = lax.axis_index("expert"), lax.axis_index("tensor"), lax.axis_index("replica")
    rows, width = tok.shape
    per = n // 2
    size = rows // 2 // pieces
    core_to, block_to = z // per, lax.rem(z, per)
    meet(x, z, r, n)

    def spot(block, core, start, count):
        columns = pl.ds(pl.multiple_of(block * width, width), width)
        return table.at[rows_at(core * rows + start, count), columns]

    def own_copy():
        return pltpu.make_async_copy(tok, spot(block_to, r, 0, rows), own_sem)

    def core_copy():
        return pltpu.make_async_remote_copy(
            src_ref=tok, dst_ref=spot(block_to, r, 0, rows), send_sem=own_send, recv_sem=own_recv,
            device_id={"replica": 1 - r}, device_id_type=MESH,
        )

    def z_copy(p, step):
        start = x * (rows // 2) + p * size
        return pltpu.make_async_remote_copy(
            src_ref=tok.at[rows_at(start, size)], dst_ref=spot(block_to, r, start, size),
            send_sem=z_send.at[p, step], recv_sem=z_recv.at[p, block_to, r],
            device_id={"tensor": lax.rem(z + step, n), "replica": core_to}, device_id_type=MESH,
        )

    def landed(p, block, core):
        place = spot(block, core, x * (rows // 2) + p * size, size)
        return pltpu.make_async_remote_copy(
            src_ref=place, dst_ref=place, send_sem=x_send.at[p, block, core], recv_sem=z_recv.at[p, block, core],
            device_id={"expert": 1 - x}, device_id_type=MESH,
        )

    def x_copy(p, block, core):
        place = spot(block, core, x * (rows // 2) + p * size, size)
        return pltpu.make_async_remote_copy(
            src_ref=place, dst_ref=place, send_sem=x_send.at[p, block, core], recv_sem=x_recv.at[p, block, core],
            device_id={"expert": 1 - x}, device_id_type=MESH,
        )

    for p in range(pieces):
        for step in range(1, n):
            z_copy(p, step).start()
    pl.when(core_to == r)(lambda: own_copy().start())
    pl.when(core_to != r)(lambda: core_copy().start())

    far = [(p, block, core) for p in range(pieces) for block in range(per) for core in range(2)]

    def forward(p, block, core):
        landed(p, block, core).wait_recv()
        x_copy(p, block, core).start()

    for p, block, core in far:
        pl.when(per * r + block != z)(functools.partial(forward, p, block, core))

    def finish(p, block, core):
        x_copy(p, block, core).wait()

    for p, block, core in far:
        pl.when(per * r + block != z)(functools.partial(finish, p, block, core))

    def finish_near():
        own_copy().wait()
        core_copy().wait_recv()

    pl.when(core_to == r)(finish_near)
    pl.when(core_to != r)(lambda: core_copy().wait_send())
    for p in range(pieces):
        for step in range(1, n):
            z_copy(p, step).wait_send()


def gather_tokens(tokens, n):
    rows, width = tokens.shape
    per, pieces = n // 2, 2
    dma = pltpu.SemaphoreType.DMA
    return pl.pallas_call(
        functools.partial(gather_kernel, n, pieces),
        out_shape=jax.ShapeDtypeStruct((2 * rows, per * width), tokens.dtype),
        in_specs=[pl.BlockSpec(memory_space=pl.ANY)],
        out_specs=pl.BlockSpec(memory_space=pl.ANY),
        scratch_shapes=[
            dma, dma, dma, dma((pieces, n)), dma((pieces, per, 2)), dma((pieces, per, 2)), dma((pieces, per, 2)),
        ],
        compiler_params=compiler_params(collective_id=0, has_side_effects=True),
    )(tokens)


def reduce_kernel(n, part, out, from_x, summed, from_z, final, x_send, x_recv, z_send, z_recv, f_send, f_recv):
    x, z, r = lax.axis_index("expert"), lax.axis_index("tensor"), lax.axis_index("replica")
    per = n // 2
    half, width = from_z.shape[1:]
    meet(x, z, r, n)

    def mine_of(side, block, core):
        return part.at[rows_at(core * 2 * half + side * half, half), pl.ds(block * width, width)]

    def x_copy(block, core):
        return pltpu.make_async_remote_copy(
            src_ref=mine_of(1 - x, block, core), dst_ref=from_x.at[block, core],
            send_sem=x_send.at[block, core], recv_sem=x_recv.at[block, core],
            device_id={"expert": 1 - x}, device_id_type=MESH,
        )

    def z_copy(block, core):
        return pltpu.make_async_remote_copy(
            src_ref=summed.at[block, core], dst_ref=from_z.at[z],
            send_sem=z_send.at[block, core], recv_sem=z_recv.at[z],
            device_id={"tensor": per * r + block, "replica": core}, device_id_type=MESH,
        )

    def arrival(source):
        return pltpu.make_async_remote_copy(
            src_ref=from_z.at[source], dst_ref=from_z.at[source],
            send_sem=z_send.at[0, 0], recv_sem=z_recv.at[source],
            device_id={"expert": 1 - x}, device_id_type=MESH,
        )

    def f_copy():
        return pltpu.make_async_remote_copy(
            src_ref=final.at[x], dst_ref=final.at[x], send_sem=f_send, recv_sem=f_recv,
            device_id={"expert": 1 - x}, device_id_type=MESH,
        )

    places = [(block, core) for block in range(per) for core in range(2)]

    def is_self(block, core):
        return (per * r + block == z) & (r == core)

    for block, core in places:
        x_copy(block, core).start()
    for block, core in places:
        x_copy(block, core).wait()
        total = mine_of(x, block, core)[...].astype(jnp.float32) + from_x[block, core].astype(jnp.float32)
        total = total.astype(jnp.bfloat16)
        summed[block, core] = total

        def keep(block=block, core=core):
            from_z[z] = summed[block, core]

        def send(block=block, core=core):
            z_copy(block, core).start()

        pl.when(is_self(block, core))(keep)
        pl.when(jnp.logical_not(is_self(block, core)))(send)
    for source in range(n):
        pl.when(jnp.logical_not((z == source) & (z // per == r)))(lambda source=source: arrival(source).wait_recv())
    total = from_z[0].astype(jnp.float32)
    for source in range(1, n):
        total = total + from_z[source].astype(jnp.float32)
    final[x] = total.astype(jnp.bfloat16)
    f_copy().start()
    for block, core in places:
        pl.when(jnp.logical_not(is_self(block, core)))(
            lambda block=block, core=core: z_copy(block, core).wait_send()
        )
    f_copy().wait()
    for side in range(2):
        out[pl.ds(side * half, half), :] = final[side]


def reduce_parts(part, n):
    rows, columns = part.shape
    per = n // 2
    half, width = rows // 4, columns // per
    dma, kind = pltpu.SemaphoreType.DMA, part.dtype
    return pl.pallas_call(
        functools.partial(reduce_kernel, n),
        out_shape=jax.ShapeDtypeStruct((rows // 2, width), kind),
        in_specs=[pl.BlockSpec(memory_space=pltpu.VMEM)],
        out_specs=pl.BlockSpec(memory_space=pltpu.VMEM),
        scratch_shapes=[
            pltpu.VMEM((per, 2, half, width), kind),
            pltpu.VMEM((per, 2, half, width), kind),
            pltpu.VMEM((n, half, width), kind),
            pltpu.VMEM((2, half, width), kind),
            dma((per, 2)), dma((per, 2)), dma((per, 2)), dma((n,)), dma, dma,
        ],
        compiler_params=compiler_params(collective_id=1, has_side_effects=True),
    )(part)


def body(tokens, w_gate, w_up, w_down, block_rows, block_gates, block_count):
    core = lax.axis_index("replica")
    token_rows = tokens.shape[0]
    experts = w_gate.shape[0]
    n_tensor = lax.axis_size("tensor")
    direct = lax.axis_size("expert") == 2 and n_tensor == 4
    ids, weight = slot_lists(block_rows, block_gates, block_count, core, token_rows)
    if direct:
        table = gather_tokens(tokens, n_tensor)
    else:
        full_rows = lax.all_gather(tokens, "tensor", axis=1, tiled=True)
        kept_rows = half_of(full_rows, 1, core)
        from_other = swap_cores(half_of(full_rows, 1, 1 - core))
        table = jnp.concatenate(
            [jnp.where(core == 0, kept_rows, from_other), jnp.where(core == 0, from_other, kept_rows)], axis=0
        )
    token_at = jnp.arange(2 * token_rows, dtype=jnp.int32)
    at = jnp.reshape(core, (1,)).astype(jnp.int32)

    routed, sums = [], []
    for e in range(experts):
        onehot = (ids[e][:, None] == token_at[None, :]).astype(jnp.bfloat16)
        routed.append(dot(onehot, table).astype(jnp.bfloat16))
        sums.append([swap_cores(p) for p in partial_sums(at, routed[e], w_gate, w_up, e)])
    hidden, hidden_other = [], []
    for e in range(experts):
        hidden.append(hidden_units(at, routed[e], w_gate, w_up, sums[e][0], sums[e][1], e))
        hidden_other.append(swap_cores(hidden[e]))
    parts = [
        weighted_down(at, hidden[e], hidden_other[e], w_down, weight[e][:, None], e) for e in range(experts)
    ]
    parts = jnp.concatenate(parts, axis=0)
    spread = (token_at[:, None] == ids.reshape(-1)[None, :]).astype(jnp.bfloat16)
    if direct:
        return reduce_parts(dot(spread, parts).astype(jnp.bfloat16), n_tensor)
    both = dot(spread, parts).astype(jnp.bfloat16)
    mine = half_of(both, 0, core)
    theirs = swap_cores(half_of(both, 0, 1 - core))
    low = jnp.where(core == 0, mine, theirs)
    high = jnp.where(core == 0, theirs, mine)
    own = lax.psum_scatter(jnp.concatenate([low, high], axis=1), "tensor", scatter_dimension=1, tiled=True)
    return lax.psum(own, "expert")


def solution(mesh):
    placed = (
        P(("groups", "replica"), "tensor"),
        P("expert", "replica", "tensor"),
        P("expert", "replica", "tensor"),
        P("expert", "tensor", "replica"),
        P("expert", ("groups", "replica"), None),
        P("expert", ("groups", "replica"), None),
        P("expert", ("groups", "replica")),
    )
    return jax.shard_map(
        body,
        mesh=mesh,
        in_specs=placed,
        out_specs=P(("groups", "replica"), "tensor"),
        check_vma=False,
    )
```

```python
import functools

import jax
import jax.numpy as jnp
from jax import lax
from jax.experimental import pallas as pl
from jax.experimental.pallas import tpu as pltpu
from jax.sharding import PartitionSpec as P

BLOCK = 128
TILE = 512
VMEM_BYTES = 48 * 1024 * 1024
MESH = pl.DeviceIdType.MESH
PAIR_BLOCKS = 6
SWAP = ((0, 1), (1, 0))


def swap_cores(x):
    return lax.ppermute(x, "replica", SWAP)


def half_of(x, axis, which):
    size = x.shape[axis] // 2
    return lax.dynamic_slice_in_dim(x, which * size, size, axis)


def dot(a, b):
    return jnp.dot(a, b, preferred_element_type=jnp.float32)


def slot_lists(block_rows, block_gates, block_count, core, token_rows):
    experts, _, slots = block_rows.shape
    blocks = slots // BLOCK
    counts = jnp.broadcast_to(block_count.astype(jnp.float32)[:, :, None], block_rows.shape)
    mine = jnp.concatenate([block_rows.astype(jnp.float32), block_gates, counts], axis=1)
    other = swap_cores(mine)
    first = jnp.where(core == 0, mine, other)
    second = jnp.where(core == 0, other, mine)
    shift = jnp.float32(token_rows)
    first_rows = first[:, 0]
    second_rows = second[:, 0] + shift
    rows = jnp.concatenate([first_rows, second_rows], axis=1).reshape(experts, 1, 2 * blocks, BLOCK)
    gates = jnp.concatenate([first[:, 1], second[:, 1]], axis=1).reshape(experts, 1, 2 * blocks, BLOCK)
    n_first = first[:, 2, :1].astype(jnp.int32)
    n_second = second[:, 2, :1].astype(jnp.int32)
    at = jnp.arange(PAIR_BLOCKS, dtype=jnp.int32)[None, :]
    source = jnp.where(at < n_first, at, blocks + at - n_first)
    source = jnp.where(at < n_first + n_second, source, -1)
    pick = source[:, :, None] == jnp.arange(2 * blocks, dtype=jnp.int32)[None, None, :]
    pick = pick[:, :, :, None]
    ids = jnp.sum(jnp.where(pick, rows, 0.0), axis=2).reshape(experts, PAIR_BLOCKS * BLOCK)
    weight = jnp.sum(jnp.where(pick, gates, 0.0), axis=2).reshape(experts, PAIR_BLOCKS * BLOCK)
    return ids.astype(jnp.int32), weight


def weight_spec(shape, e, split, which):
    if split == 2:
        tile = min(TILE, shape[2] // 2)
        per = shape[2] // 2 // tile
        return pl.BlockSpec(
            (1, shape[1], tile),
            lambda j, at: (e, 0, (at[0] if which else 1 - at[0]) * per + j),
        )
    tile = min(TILE, shape[2])
    return pl.BlockSpec((1, shape[1] // 2, tile), lambda j, at: (e, at[0] if which else 1 - at[0], j))


def whole_spec(x):
    return pl.BlockSpec(x.shape, lambda j, at: (0,) * len(x.shape))


def tiles_spec(rows, tile):
    return pl.BlockSpec((rows, tile), lambda j, at: (0, j))


def cost(rows, depth, columns):
    return pl.CostEstimate(
        flops=2 * rows * depth * columns,
        bytes_accessed=2 * (rows * depth + depth * columns + rows * columns),
        transcendentals=0,
    )


def compiler_params(**more):
    return pltpu.CompilerParams(vmem_limit_bytes=VMEM_BYTES, **more)


def partial_kernel(at, routed, gate_matrix, up_matrix, gate_out, up_out):
    gate_out[...] = dot(routed[...], gate_matrix[0]).astype(jnp.bfloat16)
    up_out[...] = dot(routed[...], up_matrix[0]).astype(jnp.bfloat16)


def partial_sums(at, routed, w_gate, w_up, e):
    rows, depth = routed.shape
    half = w_gate.shape[2] // 2
    tile = min(TILE, half)
    out = jax.ShapeDtypeStruct((rows, half), jnp.bfloat16)
    return pl.pallas_call(
        partial_kernel,
        grid_spec=pltpu.PrefetchScalarGridSpec(
            num_scalar_prefetch=1,
            grid=(half // tile,),
            in_specs=[whole_spec(routed), weight_spec(w_gate.shape, e, 2, 0), weight_spec(w_up.shape, e, 2, 0)],
            out_specs=[tiles_spec(rows, tile)] * 2,
        ),
        out_shape=[out, out],
        cost_estimate=cost(rows, depth, 2 * half),
        compiler_params=compiler_params(),
    )(at, routed, w_gate, w_up)


def hidden_kernel(at, routed, gate_matrix, up_matrix, gate_in, up_in, out):
    gate = dot(routed[...], gate_matrix[0]) + gate_in[...].astype(jnp.float32)
    up = dot(routed[...], up_matrix[0]) + up_in[...].astype(jnp.float32)
    out[...] = (gate / (1.0 + jnp.exp(-gate)) * up).astype(jnp.bfloat16)


def hidden_units(at, routed, w_gate, w_up, gate_in, up_in, e):
    rows, depth = routed.shape
    half = w_gate.shape[2] // 2
    tile = min(TILE, half)
    return pl.pallas_call(
        hidden_kernel,
        grid_spec=pltpu.PrefetchScalarGridSpec(
            num_scalar_prefetch=1,
            grid=(half // tile,),
            in_specs=[whole_spec(routed), weight_spec(w_gate.shape, e, 2, 1), weight_spec(w_up.shape, e, 2, 1)]
            + [tiles_spec(rows, tile)] * 2,
            out_specs=tiles_spec(rows, tile),
        ),
        out_shape=jax.ShapeDtypeStruct((rows, half), jnp.bfloat16),
        cost_estimate=cost(rows, depth, 2 * half),
        compiler_params=compiler_params(),
    )(at, routed, w_gate, w_up, gate_in, up_in)


def down_kernel(at, own, other, own_matrix, other_matrix, weight, out):
    summed = dot(own[...], own_matrix[0]) + dot(other[...], other_matrix[0])
    out[...] = (summed * weight[...]).astype(jnp.bfloat16)


def weighted_down(at, own, other, w_down, weight, e):
    rows, half = own.shape
    columns = w_down.shape[2]
    tile = min(TILE, columns)
    return pl.pallas_call(
        down_kernel,
        grid_spec=pltpu.PrefetchScalarGridSpec(
            num_scalar_prefetch=1,
            grid=(columns // tile,),
            in_specs=[
                whole_spec(own),
                whole_spec(other),
                weight_spec(w_down.shape, e, 1, 1),
                weight_spec(w_down.shape, e, 1, 0),
                whole_spec(weight),
            ],
            out_specs=tiles_spec(rows, tile),
        ),
        out_shape=jax.ShapeDtypeStruct((rows, columns), jnp.bfloat16),
        cost_estimate=cost(rows, 2 * half, columns),
        compiler_params=compiler_params(),
    )(at, own, other, w_down, w_down, weight)


def meet(x, z, r, n_tensor):
    barrier = pltpu.get_barrier_semaphore()
    for dz in range(n_tensor):
        for dr in range(2):
            if dz or dr:
                there = {"tensor": lax.rem(z + dz, n_tensor), "replica": lax.rem(r + dr, 2)}
                pl.semaphore_signal(barrier, inc=1, device_id=there, device_id_type=MESH)
    pl.semaphore_signal(barrier, inc=1, device_id={"expert": 1 - x}, device_id_type=MESH)
    pl.semaphore_wait(barrier, 2 * n_tensor)


def rows_at(start, size):
    return pl.ds(pl.multiple_of(start, 64), size)


def gather_kernel(n, pieces, tok, table, own_sem, own_send, own_recv, z_send, z_recv, relay_send, x_send, x_recv):
    x, z, r = lax.axis_index("expert"), lax.axis_index("tensor"), lax.axis_index("replica")
    rows, width = tok.shape
    per = n // 2
    size = rows // 2 // pieces
    core_to, block_to = z // per, lax.rem(z, per)
    meet(x, z, r, n)

    def spot(block, core, start, count):
        columns = pl.ds(pl.multiple_of(block * width, width), width)
        return table.at[rows_at(core * rows + start, count), columns]

    def own_copy():
        return pltpu.make_async_copy(tok, spot(block_to, r, 0, rows), own_sem)

    def core_copy():
        return pltpu.make_async_remote_copy(
            src_ref=tok, dst_ref=spot(block_to, r, 0, rows), send_sem=own_send, recv_sem=own_recv,
            device_id={"replica": 1 - r}, device_id_type=MESH,
        )

    def z_copy(p, way):
        start = x * (rows // 2) + p * size
        return pltpu.make_async_remote_copy(
            src_ref=tok.at[rows_at(start, size)], dst_ref=spot(block_to, r, start, size),
            send_sem=z_send.at[p, way], recv_sem=z_recv.at[p, block_to, r],
            device_id={"tensor": z - 1 + 2 * way, "replica": core_to}, device_id_type=MESH,
        )

    def relay_copy(p, block, core, way):
        place = spot(block, core, x * (rows // 2) + p * size, size)
        return pltpu.make_async_remote_copy(
            src_ref=place, dst_ref=place,
            send_sem=relay_send.at[p, block, core], recv_sem=z_recv.at[p, block, core],
            device_id={"tensor": z - 1 + 2 * way}, device_id_type=MESH,
        )

    def landed(p, block, core):
        place = spot(block, core, x * (rows // 2) + p * size, size)
        return pltpu.make_async_remote_copy(
            src_ref=place, dst_ref=place, send_sem=x_send.at[p, block, core], recv_sem=z_recv.at[p, block, core],
            device_id={"expert": 1 - x}, device_id_type=MESH,
        )

    def x_copy(p, block, core):
        place = spot(block, core, x * (rows // 2) + p * size, size)
        return pltpu.make_async_remote_copy(
            src_ref=place, dst_ref=place, send_sem=x_send.at[p, block, core], recv_sem=x_recv.at[p, block, core],
            device_id={"expert": 1 - x}, device_id_type=MESH,
        )

    onward = ((z > 0), (z < n - 1))
    for p in range(pieces):
        for way in range(2):
            pl.when(onward[way])(lambda p=p, way=way: z_copy(p, way).start())
    pl.when(core_to == r)(lambda: own_copy().start())
    pl.when(core_to != r)(lambda: core_copy().start())

    above = z // (per * (r + 1))
    far = [(p, k + above * (per - 1 - 2 * k), core) for k in range(per) for p in range(pieces) for core in range(2)]

    def passes(block, way):
        source = per * r + block
        return onward[way] & ((source < z) if way else (source > z))

    def forward(p, block, core):
        landed(p, block, core).wait_recv()
        for way in range(2):
            pl.when(passes(block, way))(lambda way=way: relay_copy(p, block, core, way).start())
        x_copy(p, block, core).start()

    for p, block, core in far:
        pl.when(per * r + block != z)(functools.partial(forward, p, block, core))

    def finish(p, block, core):
        x_copy(p, block, core).wait()
        for way in range(2):
            pl.when(passes(block, way))(lambda way=way: relay_copy(p, block, core, way).wait_send())

    for p, block, core in far:
        pl.when(per * r + block != z)(functools.partial(finish, p, block, core))

    def finish_near():
        own_copy().wait()
        core_copy().wait_recv()

    pl.when(core_to == r)(finish_near)
    pl.when(core_to != r)(lambda: core_copy().wait_send())
    for p in range(pieces):
        for way in range(2):
            pl.when(onward[way])(lambda p=p, way=way: z_copy(p, way).wait_send())


def gather_tokens(tokens, n):
    rows, width = tokens.shape
    per, pieces = n // 2, 4
    dma = pltpu.SemaphoreType.DMA
    return pl.pallas_call(
        functools.partial(gather_kernel, n, pieces),
        out_shape=jax.ShapeDtypeStruct((2 * rows, per * width), tokens.dtype),
        in_specs=[pl.BlockSpec(memory_space=pl.ANY)],
        out_specs=pl.BlockSpec(memory_space=pl.ANY),
        scratch_shapes=[
            dma, dma, dma, dma((pieces, 2)), *[dma((pieces, per, 2))] * 4,
        ],
        compiler_params=compiler_params(collective_id=0, has_side_effects=True),
    )(tokens)


def reduce_kernel(n, part, out, from_x, summed, from_z, final, x_send, x_recv, z_send, z_recv, f_send, f_recv):
    x, z, r = lax.axis_index("expert"), lax.axis_index("tensor"), lax.axis_index("replica")
    per = n // 2
    half, width = from_z.shape[1:]
    meet(x, z, r, n)

    def mine_of(side, block, core):
        return part.at[rows_at(core * 2 * half + side * half, half), pl.ds(block * width, width)]

    def x_copy(block, core):
        return pltpu.make_async_remote_copy(
            src_ref=mine_of(1 - x, block, core), dst_ref=from_x.at[block, core],
            send_sem=x_send.at[block, core], recv_sem=x_recv.at[block, core],
            device_id={"expert": 1 - x}, device_id_type=MESH,
        )

    def z_copy(block, core):
        return pltpu.make_async_remote_copy(
            src_ref=summed.at[block, core], dst_ref=from_z.at[z],
            send_sem=z_send.at[block, core], recv_sem=z_recv.at[z],
            device_id={"tensor": per * r + block, "replica": core}, device_id_type=MESH,
        )

    def arrival(source):
        return pltpu.make_async_remote_copy(
            src_ref=from_z.at[source], dst_ref=from_z.at[source],
            send_sem=z_send.at[0, 0], recv_sem=z_recv.at[source],
            device_id={"expert": 1 - x}, device_id_type=MESH,
        )

    def f_copy():
        return pltpu.make_async_remote_copy(
            src_ref=final.at[x], dst_ref=final.at[x], send_sem=f_send, recv_sem=f_recv,
            device_id={"expert": 1 - x}, device_id_type=MESH,
        )

    places = [(block, core) for block in range(per) for core in range(2)]

    def is_self(block, core):
        return (per * r + block == z) & (r == core)

    for block, core in places:
        x_copy(block, core).start()
    for block, core in places:
        x_copy(block, core).wait()
        total = mine_of(x, block, core)[...].astype(jnp.float32) + from_x[block, core].astype(jnp.float32)
        total = total.astype(jnp.bfloat16)
        summed[block, core] = total

        def keep(block=block, core=core):
            from_z[z] = summed[block, core]

        def send(block=block, core=core):
            z_copy(block, core).start()

        pl.when(is_self(block, core))(keep)
        pl.when(jnp.logical_not(is_self(block, core)))(send)
    for source in range(n):
        pl.when(jnp.logical_not((z == source) & (z // per == r)))(lambda source=source: arrival(source).wait_recv())
    total = from_z[0].astype(jnp.float32)
    for source in range(1, n):
        total = total + from_z[source].astype(jnp.float32)
    final[x] = total.astype(jnp.bfloat16)
    f_copy().start()
    for block, core in places:
        pl.when(jnp.logical_not(is_self(block, core)))(
            lambda block=block, core=core: z_copy(block, core).wait_send()
        )
    f_copy().wait()
    for side in range(2):
        out[pl.ds(side * half, half), :] = final[side]


def reduce_parts(part, n):
    rows, columns = part.shape
    per = n // 2
    half, width = rows // 4, columns // per
    dma, kind = pltpu.SemaphoreType.DMA, part.dtype
    return pl.pallas_call(
        functools.partial(reduce_kernel, n),
        out_shape=jax.ShapeDtypeStruct((rows // 2, width), kind),
        in_specs=[pl.BlockSpec(memory_space=pltpu.VMEM)],
        out_specs=pl.BlockSpec(memory_space=pltpu.VMEM),
        scratch_shapes=[
            pltpu.VMEM((per, 2, half, width), kind),
            pltpu.VMEM((per, 2, half, width), kind),
            pltpu.VMEM((n, half, width), kind),
            pltpu.VMEM((2, half, width), kind),
            dma((per, 2)), dma((per, 2)), dma((per, 2)), dma((n,)), dma, dma,
        ],
        compiler_params=compiler_params(collective_id=1, has_side_effects=True),
    )(part)


def body(tokens, w_gate, w_up, w_down, block_rows, block_gates, block_count):
    core = lax.axis_index("replica")
    token_rows = tokens.shape[0]
    experts = w_gate.shape[0]
    n_tensor = lax.axis_size("tensor")
    direct = lax.axis_size("expert") == 2 and n_tensor == 4
    ids, weight = slot_lists(block_rows, block_gates, block_count, core, token_rows)
    if direct:
        table = gather_tokens(tokens, n_tensor)
    else:
        full_rows = lax.all_gather(tokens, "tensor", axis=1, tiled=True)
        kept_rows = half_of(full_rows, 1, core)
        from_other = swap_cores(half_of(full_rows, 1, 1 - core))
        table = jnp.concatenate(
            [jnp.where(core == 0, kept_rows, from_other), jnp.where(core == 0, from_other, kept_rows)], axis=0
        )
    token_at = jnp.arange(2 * token_rows, dtype=jnp.int32)
    at = jnp.reshape(core, (1,)).astype(jnp.int32)

    routed, sums = [], []
    for e in range(experts):
        onehot = (ids[e][:, None] == token_at[None, :]).astype(jnp.bfloat16)
        routed.append(dot(onehot, table).astype(jnp.bfloat16))
        sums.append([swap_cores(p) for p in partial_sums(at, routed[e], w_gate, w_up, e)])
    hidden, hidden_other = [], []
    for e in range(experts):
        hidden.append(hidden_units(at, routed[e], w_gate, w_up, sums[e][0], sums[e][1], e))
        hidden_other.append(swap_cores(hidden[e]))
    parts = [
        weighted_down(at, hidden[e], hidden_other[e], w_down, weight[e][:, None], e) for e in range(experts)
    ]
    parts = jnp.concatenate(parts, axis=0)
    spread = (token_at[:, None] == ids.reshape(-1)[None, :]).astype(jnp.bfloat16)
    if direct:
        return reduce_parts(dot(spread, parts).astype(jnp.bfloat16), n_tensor)
    both = dot(spread, parts).astype(jnp.bfloat16)
    mine = half_of(both, 0, core)
    theirs = swap_cores(half_of(both, 0, 1 - core))
    low = jnp.where(core == 0, mine, theirs)
    high = jnp.where(core == 0, theirs, mine)
    own = lax.psum_scatter(jnp.concatenate([low, high], axis=1), "tensor", scatter_dimension=1, tiled=True)
    return lax.psum(own, "expert")


def solution(mesh):
    placed = (
        P(("groups", "replica"), "tensor"),
        P("expert", "replica", "tensor"),
        P("expert", "replica", "tensor"),
        P("expert", "tensor", "replica"),
        P("expert", ("groups", "replica"), None),
        P("expert", ("groups", "replica"), None),
        P("expert", ("groups", "replica")),
    )
    return jax.shard_map(
        body,
        mesh=mesh,
        in_specs=placed,
        out_specs=P(("groups", "replica"), "tensor"),
        check_vma=False,
    )
```

```python
import functools

import jax
import jax.numpy as jnp
from jax import lax
from jax.experimental import pallas as pl
from jax.experimental.pallas import tpu as pltpu
from jax.sharding import PartitionSpec as P

BLOCK = 128
TILE = 512
VMEM_BYTES = 48 * 1024 * 1024
MESH = pl.DeviceIdType.MESH
PAIR_BLOCKS = 6
SHORT_BLOCKS = 4
SWAP = ((0, 1), (1, 0))


def swap_cores(x):
    return lax.ppermute(x, "replica", SWAP)


def half_of(x, axis, which):
    size = x.shape[axis] // 2
    return lax.dynamic_slice_in_dim(x, which * size, size, axis)


def dot(a, b):
    return jnp.dot(a, b, preferred_element_type=jnp.float32)


def slot_lists(block_rows, block_gates, block_count, core, token_rows):
    experts, _, slots = block_rows.shape
    blocks = slots // BLOCK
    counts = jnp.broadcast_to(block_count.astype(jnp.float32)[:, :, None], block_rows.shape)
    mine = jnp.concatenate([block_rows.astype(jnp.float32), block_gates, counts], axis=1)
    other = swap_cores(mine)
    first = jnp.where(core == 0, mine, other)
    second = jnp.where(core == 0, other, mine)
    shift = jnp.float32(token_rows)
    first_rows = first[:, 0]
    second_rows = second[:, 0] + shift
    rows = jnp.concatenate([first_rows, second_rows], axis=1).reshape(experts, 1, 2 * blocks, BLOCK)
    gates = jnp.concatenate([first[:, 1], second[:, 1]], axis=1).reshape(experts, 1, 2 * blocks, BLOCK)
    n_first = first[:, 2, :1].astype(jnp.int32)
    n_second = second[:, 2, :1].astype(jnp.int32)
    at = jnp.arange(PAIR_BLOCKS, dtype=jnp.int32)[None, :]
    source = jnp.where(at < n_first, at, blocks + at - n_first)
    source = jnp.where(at < n_first + n_second, source, -1)
    pick = source[:, :, None] == jnp.arange(2 * blocks, dtype=jnp.int32)[None, None, :]
    pick = pick[:, :, :, None]
    ids = jnp.sum(jnp.where(pick, rows, 0.0), axis=2).reshape(experts, PAIR_BLOCKS * BLOCK)
    weight = jnp.sum(jnp.where(pick, gates, 0.0), axis=2).reshape(experts, PAIR_BLOCKS * BLOCK)
    return ids.astype(jnp.int32), weight, (n_first + n_second)[:, 0]


def weight_spec(shape, e, split, which):
    if split == 2:
        tile = min(TILE, shape[2] // 2)
        per = shape[2] // 2 // tile
        return pl.BlockSpec(
            (1, shape[1], tile),
            lambda j, at: (e, 0, (at[0] if which else 1 - at[0]) * per + j),
        )
    tile = min(TILE, shape[2])
    return pl.BlockSpec((1, shape[1] // 2, tile), lambda j, at: (e, at[0] if which else 1 - at[0], j))


def whole_spec(x):
    return pl.BlockSpec(x.shape, lambda j, at: (0,) * len(x.shape))


def tiles_spec(rows, tile):
    return pl.BlockSpec((rows, tile), lambda j, at: (0, j))


def cost(rows, depth, columns):
    return pl.CostEstimate(
        flops=2 * rows * depth * columns,
        bytes_accessed=2 * (rows * depth + depth * columns + rows * columns),
        transcendentals=0,
    )


def compiler_params(**more):
    return pltpu.CompilerParams(vmem_limit_bytes=VMEM_BYTES, **more)


def for_live(at, e, run):
    short = at[1 + e] <= SHORT_BLOCKS
    pl.when(short)(lambda: run(SHORT_BLOCKS * BLOCK))
    pl.when(jnp.logical_not(short))(lambda: run(PAIR_BLOCKS * BLOCK))


def partial_kernel(e, at, routed, gate_matrix, up_matrix, gate_out, up_out):
    def run(rows):
        gate_out[:rows] = dot(routed[:rows], gate_matrix[0]).astype(jnp.bfloat16)
        up_out[:rows] = dot(routed[:rows], up_matrix[0]).astype(jnp.bfloat16)

    for_live(at, e, run)


def partial_sums(at, routed, w_gate, w_up, e):
    rows, depth = routed.shape
    half = w_gate.shape[2] // 2
    tile = min(TILE, half)
    out = jax.ShapeDtypeStruct((rows, half), jnp.bfloat16)
    return pl.pallas_call(
        functools.partial(partial_kernel, e),
        grid_spec=pltpu.PrefetchScalarGridSpec(
            num_scalar_prefetch=1,
            grid=(half // tile,),
            in_specs=[whole_spec(routed), weight_spec(w_gate.shape, e, 2, 0), weight_spec(w_up.shape, e, 2, 0)],
            out_specs=[tiles_spec(rows, tile)] * 2,
        ),
        out_shape=[out, out],
        cost_estimate=cost(rows, depth, 2 * half),
        compiler_params=compiler_params(),
    )(at, routed, w_gate, w_up)


def hidden_kernel(e, at, routed, gate_matrix, up_matrix, gate_in, up_in, out):
    def run(rows):
        gate = dot(routed[:rows], gate_matrix[0]) + gate_in[:rows].astype(jnp.float32)
        up = dot(routed[:rows], up_matrix[0]) + up_in[:rows].astype(jnp.float32)
        out[:rows] = (gate / (1.0 + jnp.exp(-gate)) * up).astype(jnp.bfloat16)

    for_live(at, e, run)


def hidden_units(at, routed, w_gate, w_up, gate_in, up_in, e):
    rows, depth = routed.shape
    half = w_gate.shape[2] // 2
    tile = min(TILE, half)
    return pl.pallas_call(
        functools.partial(hidden_kernel, e),
        grid_spec=pltpu.PrefetchScalarGridSpec(
            num_scalar_prefetch=1,
            grid=(half // tile,),
            in_specs=[whole_spec(routed), weight_spec(w_gate.shape, e, 2, 1), weight_spec(w_up.shape, e, 2, 1)]
            + [tiles_spec(rows, tile)] * 2,
            out_specs=tiles_spec(rows, tile),
        ),
        out_shape=jax.ShapeDtypeStruct((rows, half), jnp.bfloat16),
        cost_estimate=cost(rows, depth, 2 * half),
        compiler_params=compiler_params(),
    )(at, routed, w_gate, w_up, gate_in, up_in)


def down_kernel(e, at, own, other, own_matrix, other_matrix, weight, out):
    def run(rows):
        summed = dot(own[:rows], own_matrix[0]) + dot(other[:rows], other_matrix[0])
        out[:rows] = (summed * weight[:rows]).astype(jnp.bfloat16)
        if rows < out.shape[0]:
            out[rows:] = jnp.zeros((out.shape[0] - rows, out.shape[1]), out.dtype)

    for_live(at, e, run)


def weighted_down(at, own, other, w_down, weight, e):
    rows, half = own.shape
    columns = w_down.shape[2]
    tile = min(TILE, columns)
    return pl.pallas_call(
        functools.partial(down_kernel, e),
        grid_spec=pltpu.PrefetchScalarGridSpec(
            num_scalar_prefetch=1,
            grid=(columns // tile,),
            in_specs=[
                whole_spec(own),
                whole_spec(other),
                weight_spec(w_down.shape, e, 1, 1),
                weight_spec(w_down.shape, e, 1, 0),
                whole_spec(weight),
            ],
            out_specs=tiles_spec(rows, tile),
        ),
        out_shape=jax.ShapeDtypeStruct((rows, columns), jnp.bfloat16),
        cost_estimate=cost(rows, 2 * half, columns),
        compiler_params=compiler_params(),
    )(at, own, other, w_down, w_down, weight)


def meet(x, z, r, n_tensor):
    barrier = pltpu.get_barrier_semaphore()
    for dz in range(n_tensor):
        for dr in range(2):
            if dz or dr:
                there = {"tensor": lax.rem(z + dz, n_tensor), "replica": lax.rem(r + dr, 2)}
                pl.semaphore_signal(barrier, inc=1, device_id=there, device_id_type=MESH)
    pl.semaphore_signal(barrier, inc=1, device_id={"expert": 1 - x}, device_id_type=MESH)
    pl.semaphore_wait(barrier, 2 * n_tensor)


def rows_at(start, size):
    return pl.ds(pl.multiple_of(start, 64), size)


def gather_kernel(n, pieces, tok, table, own_sem, own_send, own_recv, z_send, z_recv, relay_send, x_send, x_recv):
    x, z, r = lax.axis_index("expert"), lax.axis_index("tensor"), lax.axis_index("replica")
    rows, width = tok.shape
    per = n // 2
    size = rows // 2 // pieces
    core_to, block_to = z // per, lax.rem(z, per)
    meet(x, z, r, n)

    def spot(block, core, start, count):
        columns = pl.ds(pl.multiple_of(block * width, width), width)
        return table.at[rows_at(core * rows + start, count), columns]

    def own_copy():
        return pltpu.make_async_copy(tok, spot(block_to, r, 0, rows), own_sem)

    def core_copy():
        return pltpu.make_async_remote_copy(
            src_ref=tok, dst_ref=spot(block_to, r, 0, rows), send_sem=own_send, recv_sem=own_recv,
            device_id={"replica": 1 - r}, device_id_type=MESH,
        )

    def z_copy(p, way):
        start = x * (rows // 2) + p * size
        return pltpu.make_async_remote_copy(
            src_ref=tok.at[rows_at(start, size)], dst_ref=spot(block_to, r, start, size),
            send_sem=z_send.at[p, way], recv_sem=z_recv.at[p, block_to, r],
            device_id={"tensor": z - 1 + 2 * way, "replica": core_to}, device_id_type=MESH,
        )

    def relay_copy(p, block, core, way):
        place = spot(block, core, x * (rows // 2) + p * size, size)
        return pltpu.make_async_remote_copy(
            src_ref=place, dst_ref=place,
            send_sem=relay_send.at[p, block, core], recv_sem=z_recv.at[p, block, core],
            device_id={"tensor": z - 1 + 2 * way}, device_id_type=MESH,
        )

    def landed(p, block, core):
        place = spot(block, core, x * (rows // 2) + p * size, size)
        return pltpu.make_async_remote_copy(
            src_ref=place, dst_ref=place, send_sem=x_send.at[p, block, core], recv_sem=z_recv.at[p, block, core],
            device_id={"expert": 1 - x}, device_id_type=MESH,
        )

    def x_copy(p, block, core):
        place = spot(block, core, x * (rows // 2) + p * size, size)
        return pltpu.make_async_remote_copy(
            src_ref=place, dst_ref=place, send_sem=x_send.at[p, block, core], recv_sem=x_recv.at[p, block, core],
            device_id={"expert": 1 - x}, device_id_type=MESH,
        )

    onward = ((z > 0), (z < n - 1))
    for p in range(pieces):
        for way in range(2):
            pl.when(onward[way])(lambda p=p, way=way: z_copy(p, way).start())
    pl.when(core_to == r)(lambda: own_copy().start())
    pl.when(core_to != r)(lambda: core_copy().start())

    above = z // (per * (r + 1))
    far = [(p, k + above * (per - 1 - 2 * k), core) for k in range(per) for p in range(pieces) for core in range(2)]

    def passes(block, way):
        source = per * r + block
        return onward[way] & ((source < z) if way else (source > z))

    def forward(p, block, core):
        landed(p, block, core).wait_recv()
        for way in range(2):
            pl.when(passes(block, way))(lambda way=way: relay_copy(p, block, core, way).start())
        x_copy(p, block, core).start()

    for p, block, core in far:
        pl.when(per * r + block != z)(functools.partial(forward, p, block, core))

    def finish(p, block, core):
        x_copy(p, block, core).wait()
        for way in range(2):
            pl.when(passes(block, way))(lambda way=way: relay_copy(p, block, core, way).wait_send())

    for p, block, core in far:
        pl.when(per * r + block != z)(functools.partial(finish, p, block, core))

    def finish_near():
        own_copy().wait()
        core_copy().wait_recv()

    pl.when(core_to == r)(finish_near)
    pl.when(core_to != r)(lambda: core_copy().wait_send())
    for p in range(pieces):
        for way in range(2):
            pl.when(onward[way])(lambda p=p, way=way: z_copy(p, way).wait_send())


def gather_tokens(tokens, n):
    rows, width = tokens.shape
    per, pieces = n // 2, 4
    dma = pltpu.SemaphoreType.DMA
    return pl.pallas_call(
        functools.partial(gather_kernel, n, pieces),
        out_shape=jax.ShapeDtypeStruct((2 * rows, per * width), tokens.dtype),
        in_specs=[pl.BlockSpec(memory_space=pl.ANY)],
        out_specs=pl.BlockSpec(memory_space=pl.ANY),
        scratch_shapes=[
            dma, dma, dma, dma((pieces, 2)), *[dma((pieces, per, 2))] * 4,
        ],
        compiler_params=compiler_params(collective_id=0, has_side_effects=True),
    )(tokens)


def reduce_kernel(n, pieces, part, out, from_x, summed, from_z, final, x_send, x_recv, z_send, z_recv, f_send, f_recv):
    x, z, r = lax.axis_index("expert"), lax.axis_index("tensor"), lax.axis_index("replica")
    per = n // 2
    half, width = pieces * from_z.shape[2], from_z.shape[3]
    meet(x, z, r, n)

    size = half // pieces

    def mine_of(side, p, block, core):
        start = core * 2 * half + side * half + p * size
        return part.at[rows_at(start, size), pl.ds(block * width, width)]

    def x_copy(p, block, core):
        return pltpu.make_async_remote_copy(
            src_ref=mine_of(1 - x, p, block, core), dst_ref=from_x.at[p, block, core],
            send_sem=x_send.at[p, block, core], recv_sem=x_recv.at[p, block, core],
            device_id={"expert": 1 - x}, device_id_type=MESH,
        )

    def z_copy(p, block, core):
        return pltpu.make_async_remote_copy(
            src_ref=summed.at[p, block, core], dst_ref=from_z.at[p, z],
            send_sem=z_send.at[p, block, core], recv_sem=z_recv.at[p, z],
            device_id={"tensor": per * r + block, "replica": core}, device_id_type=MESH,
        )

    def arrival(p, source):
        return pltpu.make_async_remote_copy(
            src_ref=from_z.at[p, source], dst_ref=from_z.at[p, source],
            send_sem=z_send.at[p, 0, 0], recv_sem=z_recv.at[p, source],
            device_id={"expert": 1 - x}, device_id_type=MESH,
        )

    def f_copy(p):
        return pltpu.make_async_remote_copy(
            src_ref=final.at[x, p], dst_ref=final.at[x, p], send_sem=f_send.at[p], recv_sem=f_recv.at[p],
            device_id={"expert": 1 - x}, device_id_type=MESH,
        )

    places = [(p, block, core) for p in range(pieces) for block in range(per) for core in range(2)]

    def is_self(block, core):
        return (per * r + block == z) & (r == core)

    for p, block, core in places:
        x_copy(p, block, core).start()
    for p, block, core in places:
        x_copy(p, block, core).wait()
        total = mine_of(x, p, block, core)[...].astype(jnp.float32) + from_x[p, block, core].astype(jnp.float32)
        summed[p, block, core] = total.astype(jnp.bfloat16)

        def keep(p=p, block=block, core=core):
            from_z[p, z] = summed[p, block, core]

        def send(p=p, block=block, core=core):
            z_copy(p, block, core).start()

        pl.when(is_self(block, core))(keep)
        pl.when(jnp.logical_not(is_self(block, core)))(send)
    for p in range(pieces):
        for source in range(n):
            pl.when(jnp.logical_not((z == source) & (z // per == r)))(
                lambda p=p, source=source: arrival(p, source).wait_recv()
            )
        total = from_z[p, 0].astype(jnp.float32)
        for source in range(1, n):
            total = total + from_z[p, source].astype(jnp.float32)
        final[x, p] = total.astype(jnp.bfloat16)
        f_copy(p).start()
    for p, block, core in places:
        pl.when(jnp.logical_not(is_self(block, core)))(
            lambda p=p, block=block, core=core: z_copy(p, block, core).wait_send()
        )
    for p in range(pieces):
        f_copy(p).wait()
    for side in range(2):
        for p in range(pieces):
            out[pl.ds(side * half + p * size, size), :] = final[side, p]


def reduce_parts(part, n):
    rows, columns = part.shape
    per = n // 2
    half, width, pieces = rows // 4, columns // per, 2
    size = half // pieces
    dma, kind = pltpu.SemaphoreType.DMA, part.dtype
    return pl.pallas_call(
        functools.partial(reduce_kernel, n, pieces),
        out_shape=jax.ShapeDtypeStruct((rows // 2, width), kind),
        in_specs=[pl.BlockSpec(memory_space=pltpu.VMEM)],
        out_specs=pl.BlockSpec(memory_space=pltpu.VMEM),
        scratch_shapes=[
            pltpu.VMEM((pieces, per, 2, size, width), kind),
            pltpu.VMEM((pieces, per, 2, size, width), kind),
            pltpu.VMEM((pieces, n, size, width), kind),
            pltpu.VMEM((2, pieces, size, width), kind),
            dma((pieces, per, 2)), dma((pieces, per, 2)), dma((pieces, per, 2)), dma((pieces, n)),
            dma((pieces,)), dma((pieces,)),
        ],
        compiler_params=compiler_params(collective_id=1, has_side_effects=True),
    )(part)


def body(tokens, w_gate, w_up, w_down, block_rows, block_gates, block_count):
    core = lax.axis_index("replica")
    token_rows = tokens.shape[0]
    experts = w_gate.shape[0]
    n_tensor = lax.axis_size("tensor")
    direct = lax.axis_size("expert") == 2 and n_tensor == 4
    ids, weight, live = slot_lists(block_rows, block_gates, block_count, core, token_rows)
    if direct:
        table = gather_tokens(tokens, n_tensor)
    else:
        full_rows = lax.all_gather(tokens, "tensor", axis=1, tiled=True)
        kept_rows = half_of(full_rows, 1, core)
        from_other = swap_cores(half_of(full_rows, 1, 1 - core))
        table = jnp.concatenate(
            [jnp.where(core == 0, kept_rows, from_other), jnp.where(core == 0, from_other, kept_rows)], axis=0
        )
    token_at = jnp.arange(2 * token_rows, dtype=jnp.int32)
    at = jnp.concatenate([jnp.reshape(core, (1,)).astype(jnp.int32), live])

    routed, sums = [], []
    for e in range(experts):
        onehot = (ids[e][:, None] == token_at[None, :]).astype(jnp.bfloat16)
        routed.append(dot(onehot, table).astype(jnp.bfloat16))
        sums.append([swap_cores(p) for p in partial_sums(at, routed[e], w_gate, w_up, e)])
    hidden, hidden_other = [], []
    for e in range(experts):
        hidden.append(hidden_units(at, routed[e], w_gate, w_up, sums[e][0], sums[e][1], e))
        hidden_other.append(swap_cores(hidden[e]))
    parts = [
        weighted_down(at, hidden[e], hidden_other[e], w_down, weight[e][:, None], e) for e in range(experts)
    ]
    parts = jnp.concatenate(parts, axis=0)
    spread = (token_at[:, None] == ids.reshape(-1)[None, :]).astype(jnp.bfloat16)
    if direct:
        return reduce_parts(dot(spread, parts).astype(jnp.bfloat16), n_tensor)
    both = dot(spread, parts).astype(jnp.bfloat16)
    mine = half_of(both, 0, core)
    theirs = swap_cores(half_of(both, 0, 1 - core))
    low = jnp.where(core == 0, mine, theirs)
    high = jnp.where(core == 0, theirs, mine)
    own = lax.psum_scatter(jnp.concatenate([low, high], axis=1), "tensor", scatter_dimension=1, tiled=True)
    return lax.psum(own, "expert")


def solution(mesh):
    placed = (
        P(("groups", "replica"), "tensor"),
        P("expert", "replica", "tensor"),
        P("expert", "replica", "tensor"),
        P("expert", "tensor", "replica"),
        P("expert", ("groups", "replica"), None),
        P("expert", ("groups", "replica"), None),
        P("expert", ("groups", "replica")),
    )
    return jax.shard_map(
        body,
        mesh=mesh,
        in_specs=placed,
        out_specs=P(("groups", "replica"), "tensor"),
        check_vma=False,
    )
```
